32 devices in a mesh: dp: 4 (over y, core), seq: 8 (over z, x).
Axes of the slice: x: 2, y: 2, z: 4, core: 2. Of those that a mesh axis runs over, the one named last changes fastest.
Arguments:
- inputs: bfloat16 [4, 32768, 768], P('dp', 'seq'), may hold values from -6 to 6
- cotangent: bfloat16 [4, 32768, 768], P('dp', 'seq'), may hold values from -6 to 6
- first_factor: bfloat16 [256, 128, 256], P('dp', 'seq'), may hold values from -0.375 to 0.375
- second_factor: bfloat16 [128, 256, 128], P('dp', 'seq'), may hold values from -0.5 to 0.5
Outputs:
- grad_input: bfloat16 [4, 32768, 768], P('dp', 'seq')
- first_grad: float32 [256, 128, 256], P('dp', 'seq')
- latter_matrix_derivative: float32 [128, 256, 128], P('dp', 'seq')
The draws below stay inside these ranges and needn't reach their ends.
All inputs are finite; a program needn't handle non-finite values.
Results may differ from the reference program's by a relative error of at most 0.0085.
Values may be sent and summed in bfloat16 or wider, within the bound.
No kernel may reach another device: no remote copies, remote signals or barrier semaphores. Data moves between devices by JAX's collectives and lax.ppermute only.
A program may use at most 128 MiB of HBM per device.

```python
import jax
import jax.numpy as jnp
from jax import lax

CHANNEL_WIDTH = 768
P1 = 256
P2 = 128
SEQUENCE_LENGTH = 32768
BATCH = 4


def block_levels(key, dims, cuts, smallest, high):
    def one(dim, shards_of):
        draws = jax.random.uniform(jax.random.fold_in(jax.random.fold_in(key, 6), dim), (shards_of,), jnp.float32, smallest / len(cuts), high / len(cuts))
        return jnp.repeat(jnp.exp(draws), dims[dim] // shards_of).reshape((-1,) + (1,) * (len(dims) - dim - 1))

    loudness = one(*cuts[0])
    for cut in cuts[1:]:
        loudness = loudness * one(*cut)
    return loudness


def bell_draw(key, extent, width, most, cuts=(), held_as=jnp.bfloat16):
    factor_of = block_levels(key, extent, cuts, -0.22, 0.18) if cuts else 1.0
    drawn = jax.random.normal(key, extent, jnp.float32) * width * factor_of
    return jnp.minimum(jnp.maximum(drawn, -most), most).astype(held_as)


def setup_inputs(seed: int = 0) -> dict:
    keys = jax.random.split(jax.random.key(seed), 5)
    inputs = bell_draw(keys[0], (BATCH, SEQUENCE_LENGTH, CHANNEL_WIDTH), 1.0, 6.0, ((0, 4), (1, 8)))
    cotangent = bell_draw(keys[1], (BATCH, SEQUENCE_LENGTH, CHANNEL_WIDTH), 1.0, 6.0, ((0, 4), (1, 8)))
    first_factor = bell_draw(keys[2], (P1, P2, P1), P1 ** -0.5, 0.375, ((0, 4), (1, 8)))
    second_factor = bell_draw(keys[3], (P2, P1, P2), P2 ** -0.5, 0.5, ((0, 4), (1, 8)))
    return dict(inputs=inputs, cotangent=cotangent, first_factor=first_factor, second_factor=second_factor)


def silu_slope(values):
    logistic = jax.nn.sigmoid(values)
    return logistic * (1.0 + values * (1.0 - logistic))


def reference(inputs, cotangent, first_factor, second_factor):
    leading_entire_span = first_factor.astype(jnp.float32)
    second_wide = second_factor.astype(jnp.float32)

    def single_token_series(carry, pair):
        first_factor_sum, second_sum = carry
        tokens, upstream_in = pair
        tile_lattice = tokens.reshape(P2, P1, CHANNEL_WIDTH).astype(jnp.float32)
        line_combined_result = jnp.einsum('ibt,btf->bif', leading_entire_span, tile_lattice).astype(jnp.bfloat16)
        mixed_wide = line_combined_result.astype(jnp.float32)
        product = jnp.einsum('ijk,kjd->ijd', second_wide, mixed_wide).astype(jnp.bfloat16)
        input_wide = tokens.astype(jnp.float32)
        cot_wide = upstream_in.astype(jnp.float32)
        output_wide = product.reshape(SEQUENCE_LENGTH, CHANNEL_WIDTH).astype(jnp.float32)
        upstream = (cot_wide * jax.nn.silu(input_wide)).astype(jnp.bfloat16)
        gate_term = (cot_wide * output_wide * silu_slope(input_wide)).astype(jnp.bfloat16)
        derivative_columns_local = upstream.reshape(P2, P1, CHANNEL_WIDTH).astype(jnp.float32)
        second_sum = second_sum + jnp.einsum('ijd,kjd->ijk', derivative_columns_local, mixed_wide)
        mixed_grad = jnp.einsum('ijk,ijd->kjd', second_wide, derivative_columns_local).astype(jnp.bfloat16)
        gradient_full_width = mixed_grad.astype(jnp.float32)
        first_factor_sum = first_factor_sum + jnp.einsum('pue,pge->upg', gradient_full_width, tile_lattice)
        block_folded = jnp.einsum('wpc,pwf->pcf', leading_entire_span, gradient_full_width).reshape(SEQUENCE_LENGTH, CHANNEL_WIDTH)
        grad_tokens = (block_folded + gate_term.astype(jnp.float32)).astype(jnp.bfloat16)
        return (first_factor_sum, second_sum), grad_tokens

    start_sums = (jnp.zeros((P1, P2, P1), jnp.float32), jnp.zeros((P2, P1, P2), jnp.float32))
    sums, grad_input = lax.scan(single_token_series, start_sums, (inputs, cotangent))
    return grad_input, sums[0] / BATCH, sums[1] / BATCH
```

```python
import jax
import jax.numpy as jnp
from jax import lax
from jax.sharding import PartitionSpec as P

LEVELS = 4
PARTS = 3
AXES = ("dp", "seq")


def silu_slope(values):
    logistic = jax.nn.sigmoid(values)
    return logistic * (1.0 + values * (1.0 - logistic))


def body(inputs, cotangent, first_factor, second_factor):
    dp, seq = lax.axis_size("dp"), lax.axis_size("seq")
    ys, xs = dp // 2, seq // LEVELS
    group = 2 * xs
    sequences, tokens, channels = inputs.shape
    assert sequences == 1 and dp % 2 == 0 and seq % LEVELS == 0
    rows1, blocks, size1 = first_factor.shape
    rows2, places, size2 = second_factor.shape
    half = channels // 2
    part = half // PARTS
    mean_weight = 1.0 / (sequences * dp)

    def flat(y, c, z, x):
        return (2 * y + c) * seq + z * xs + x

    def pairs(to):
        return [
            (flat(y, c, z, x), flat(*to(y, c, z, x)))
            for y in range(ys)
            for c in range(2)
            for z in range(LEVELS)
            for x in range(xs)
        ]

    def permute(value, perm):
        return lax.ppermute(value, AXES, perm)

    there = [pairs(lambda y, c, z, x: (y, z % 2, 2 * c + (k ^ (z // 2)), x)) for k in range(2)]
    back = [[(b, a) for a, b in perm] for perm in there]
    swap = pairs(lambda y, c, z, x: (y, z % 2, 2 * (z // 2) + c, x))
    far = pairs(lambda y, c, z, x: (y, c, z ^ 2, x))
    near = pairs(lambda y, c, z, x: (y, c, z ^ 1, x))
    groups = [
        [flat(y, c, z, x) for c in range(2) for x in range(xs)]
        for y in range(ys)
        for z in range(LEVELS)
    ]

    me_y = lax.axis_index("dp") // 2
    me_z = lax.axis_index("seq") // xs
    hi, lo = me_z // 2, me_z % 2

    def ordered(mine, other, bit, axis=0):
        return jnp.where(
            bit == 0, jnp.stack([mine, other], axis), jnp.stack([other, mine], axis)
        )

    def gather(piece, by_slot):
        mine = permute(piece, swap)
        bit = hi ^ lo if by_slot else hi
        mine = ordered(mine, permute(mine, far), bit)
        sent = mine[::-1] if by_slot else mine
        mine = ordered(mine, permute(sent, near), lo)
        step = 1
        while step < ys:
            other = permute(mine, pairs(lambda y, c, z, x: (y ^ step, c, z, x)))
            mine = ordered(mine, other, (me_y // step) % 2)
            step *= 2
        return mine.reshape((dp, 2) + piece.shape)

    def choose(pair, bit):
        return jnp.where(bit == 0, pair[0], pair[1])

    def reduce(whole, by_slot):
        mine = whole.reshape((2,) * (ys.bit_length() - 1) + (2, 2) + whole.shape[2:])
        step = ys // 2
        while step >= 1:
            bit = (me_y // step) % 2
            sent = choose((mine[1], mine[0]), bit).astype(jnp.bfloat16)
            kept = choose((mine[0], mine[1]), bit)
            mine = kept + permute(
                sent, pairs(lambda y, c, z, x: (y ^ step, c, z, x))
            ).astype(jnp.float32)
            step //= 2
        sent = choose((mine[1], mine[0]), lo).astype(jnp.bfloat16)
        sent = sent[::-1] if by_slot else sent
        mine = choose((mine[0], mine[1]), lo) + permute(sent, near).astype(jnp.float32)
        bit = hi ^ lo if by_slot else hi
        sent = choose((mine[1], mine[0]), bit).astype(jnp.bfloat16)
        mine = choose((mine[0], mine[1]), bit) + permute(sent, far).astype(jnp.float32)
        return permute(mine.astype(jnp.bfloat16), swap).astype(jnp.float32)

    def to_columns(value):
        value = value.reshape(2, blocks, 2, group, places, part)
        value = lax.all_to_all(value, AXES, 3, 1, axis_index_groups=groups)
        return value.reshape(size2, 2 * places, part)

    def to_rows(value):
        value = value.reshape(2, group, blocks, 2, places, part)
        value = lax.all_to_all(value, AXES, 1, 3, axis_index_groups=groups)
        return value.reshape(2 * blocks, size1, part)

    def half_swap(value, axes):
        swapped = value
        for axis in axes:
            first, second = jnp.split(swapped, 2, axis)
            swapped = jnp.concatenate([second, first], axis)
        return jnp.where(lo == 0, value, swapped)

    first = gather(first_factor.transpose(1, 0, 2), True)
    first = first.transpose(1, 2, 0, 3, 4).reshape(2 * blocks, size1, size1)
    second = gather(second_factor.transpose(1, 0, 2), False)
    second = second.transpose(1, 2, 0, 3, 4).reshape(2 * places, size2, size2)
    second = half_swap(second, (1, 2))

    def bring(array, q):
        array = array.reshape(blocks, size1, channels)
        slots = []
        for k in range(2):
            start = (k ^ hi) * half + q * part
            piece = lax.dynamic_slice(array, (0, 0, start), (blocks, size1, part))
            slots.append(permute(piece, there[k]))
        return jnp.concatenate(slots, 0)

    x_parts = [bring(inputs, q) for q in range(PARTS)]
    c_parts = [bring(cotangent, q) for q in range(PARTS)]

    first_sum, second_sum, returned = 0.0, 0.0, []
    wide = dict(preferred_element_type=jnp.float32)
    for x_part, c_part in zip(x_parts, c_parts):
        mixed = jnp.einsum("bik,bkd->bid", first, x_part, **wide).astype(jnp.bfloat16)
        columns = to_columns(mixed)
        product = jnp.einsum("jik,kjd->ijd", second, columns, **wide).astype(jnp.bfloat16)
        output = to_rows(product)
        x_wide, c_wide = x_part.astype(jnp.float32), c_part.astype(jnp.float32)
        upstream = (c_wide * jax.nn.silu(x_wide)).astype(jnp.bfloat16)
        up_columns = to_columns(upstream)
        back_columns = jnp.einsum("jik,ijd->kjd", second, up_columns, **wide).astype(jnp.bfloat16)
        mixed_grad = to_rows(back_columns)
        second_sum += jnp.einsum("ijd,kjd->jik", up_columns, columns, **wide)
        first_sum += jnp.einsum("bid,bkd->bik", mixed_grad, x_part, **wide)
        gate_term = (c_wide * output.astype(jnp.float32) * silu_slope(x_wide)).astype(jnp.bfloat16)
        folded = jnp.einsum("bik,bid->bkd", first, mixed_grad, **wide)
        grad = (folded + gate_term.astype(jnp.float32)).astype(jnp.bfloat16)
        grad = grad.reshape(2, blocks, size1, part)
        returned.append([permute(grad[k], back[k]) for k in range(2)])

    first_sum = (first_sum * mean_weight).reshape(2, blocks, dp, rows1, size1)
    first_grad = reduce(first_sum.transpose(2, 0, 1, 3, 4), True).transpose(1, 0, 2)
    second_sum = half_swap(second_sum * mean_weight, (1, 2)).reshape(2, places, dp, rows2, size2)
    second_grad = reduce(second_sum.transpose(2, 0, 1, 3, 4), False).transpose(1, 0, 2)
    slots = [jnp.concatenate([r[k] for r in returned], -1) for k in range(2)]
    grad_input = jnp.where(
        hi == 0, jnp.concatenate(slots, -1), jnp.concatenate(slots[::-1], -1)
    ).reshape(1, tokens, channels)
    return (grad_input, first_grad, second_grad)


def solution(mesh):
    placed = P("dp", "seq", None)
    return jax.shard_map(
        body,
        mesh=mesh,
        in_specs=(placed,) * 4,
        out_specs=(placed,) * 3,
        check_vma=False,
    )
```

```python
import jax
import jax.numpy as jnp
from jax import lax
from jax.experimental import pallas as pl
from jax.experimental.pallas import tpu as pltpu
from jax.sharding import PartitionSpec as P

MANY = 2
ROOM = pltpu.CompilerParams(vmem_limit_bytes=56 * 1024 * 1024)


def upstream_kernel(x_ref, c_ref, out_ref):
    owners, many, places, channels = out_ref.shape
    for n in range(many):
        x, c = x_ref[n].astype(jnp.float32), c_ref[n].astype(jnp.float32)
        half = 0.5 * x
        up = c * (half + half * jnp.tanh(half))
        out_ref[:, n] = up.reshape(owners, places, channels).astype(out_ref.dtype)


def upstream_for_owners(x, c, owners):
    blocks, size, channels = x.shape
    row = pl.BlockSpec((MANY, size, channels), lambda b: (b, 0, 0))
    return pl.pallas_call(
        upstream_kernel,
        grid=(blocks // MANY,),
        in_specs=[row, row],
        out_specs=pl.BlockSpec((owners, MANY, size // owners, channels), lambda b: (0, b, 0, 0)),
        out_shape=jax.ShapeDtypeStruct((owners, blocks, size // owners, channels), x.dtype),
        cost_estimate=pl.CostEstimate(
            flops=8 * x.size, bytes_accessed=6 * x.size, transcendentals=x.size
        ),
        compiler_params=ROOM,
        name="upstream",
    )(x, c)


def final_kernel(y_ref, slope_ref, folded_ref, out_ref):
    many, size, channels = out_ref.shape
    for n in range(many):
        y = y_ref[:, n].reshape(size, channels)
        out_ref[n] = folded_ref[n] + y * slope_ref[n]


def final(y, slope, folded):
    blocks, size, channels = slope.shape
    owners = y.shape[0]
    row = pl.BlockSpec((MANY, size, channels), lambda b: (b, 0, 0))
    return pl.pallas_call(
        final_kernel,
        grid=(blocks // MANY,),
        in_specs=[
            pl.BlockSpec((owners, MANY, size // owners, channels), lambda b: (0, b, 0, 0)),
            row,
            row,
        ],
        out_specs=row,
        out_shape=jax.ShapeDtypeStruct(slope.shape, slope.dtype),
        cost_estimate=pl.CostEstimate(
            flops=2 * y.size, bytes_accessed=8 * y.size, transcendentals=0
        ),
        compiler_params=ROOM,
        name="final",
    )(y, slope, folded)


def tie_kernel(*refs):
    del refs


def tie(*values):
    anywhere = [pl.BlockSpec(memory_space=pl.ANY)] * len(values)
    return pl.pallas_call(
        tie_kernel,
        in_specs=anywhere,
        out_specs=anywhere,
        out_shape=[jax.ShapeDtypeStruct(v.shape, v.dtype) for v in values],
        input_output_aliases={n: n for n in range(len(values))},
        cost_estimate=pl.CostEstimate(flops=0, bytes_accessed=0, transcendentals=0),
        compiler_params=ROOM,
        name="tie",
    )(*values)


def body(inputs, cotangent, first_factor, second_factor):
    sequences, tokens, channels = inputs.shape
    assert sequences == 1
    owners = lax.axis_size("seq")
    row_block, blocks, size1 = first_factor.shape
    places = size1 // owners
    mean_weight = 1.0 / (sequences * lax.axis_size("dp"))
    bf16, wide = jnp.bfloat16, dict(preferred_element_type=jnp.float32)
    x = inputs.reshape(blocks, size1, channels)
    c = cotangent.reshape(blocks, size1, channels)

    def exchange(value):
        return lax.all_to_all(value, "seq", 0, 0, tiled=True)

    def to_columns(value):
        return exchange(value).reshape(owners * blocks, places, channels)

    def by_owner(value):
        return value.reshape(blocks, owners, places, channels).transpose(1, 0, 2, 3)

    first = lax.all_gather(first_factor, "dp", axis=0, tiled=True)
    second = lax.all_gather(second_factor, "dp", axis=0, tiled=True)
    up_columns = to_columns(upstream_for_owners(x, c, owners))
    mixed = by_owner(jnp.einsum("ibk,bkd->bid", first, x, **wide).astype(bf16))
    up_columns, mixed = tie(up_columns, mixed)
    columns = to_columns(mixed)
    back_columns = jnp.einsum("ijk,ijd->kjd", second, up_columns, **wide).astype(bf16)
    columns, back_columns = tie(columns, back_columns)
    mixed_grad = exchange(back_columns.reshape(owners, blocks, places, channels))
    product = jnp.einsum("ijk,kjd->ijd", second, columns, **wide).astype(bf16)
    mixed_grad, product = tie(mixed_grad, product)
    output = exchange(product.reshape(owners, blocks, places, channels))
    mixed_grad = mixed_grad.transpose(1, 0, 2, 3).reshape(blocks, size1, channels)
    second_grad = lax.psum_scatter(
        jnp.einsum("ijd,kjd->ijk", up_columns, columns, **wide) * mean_weight,
        "dp",
        scatter_dimension=0,
        tiled=True,
    )
    folded = jnp.einsum("ibk,bid->bkd", first, mixed_grad, **wide).astype(bf16)
    x_wide = x.astype(jnp.float32)
    logistic = jax.nn.sigmoid(x_wide)
    slope = (c.astype(jnp.float32) * logistic * (1.0 + x_wide * (1.0 - logistic))).astype(bf16)
    first_grad = lax.psum_scatter(
        jnp.einsum("bid,bkd->ibk", mixed_grad, x, **wide) * mean_weight,
        "dp",
        scatter_dimension=0,
        tiled=True,
    )
    grad_input = final(output, slope, folded).reshape(inputs.shape)
    return (grad_input, first_grad, second_grad)


def solution(mesh):
    placed = P("dp", "seq", None)
    return jax.shard_map(
        body,
        mesh=mesh,
        in_specs=(placed,) * 4,
        out_specs=(placed,) * 3,
        check_vma=False,
    )
```

```python
import jax
import jax.numpy as jnp
from jax import lax
from jax.experimental import pallas as pl
from jax.experimental.pallas import tpu as pltpu
from jax.sharding import PartitionSpec as P

MANY = 4
ROOM = pltpu.CompilerParams(vmem_limit_bytes=56 * 1024 * 1024)


def upstream_kernel(x_ref, c_ref, out_ref):
    owners, many, places, channels = out_ref.shape
    for n in range(many):
        x, c = x_ref[n].astype(jnp.float32), c_ref[n].astype(jnp.float32)
        half = 0.5 * x
        up = c * (half + half * jnp.tanh(half))
        out_ref[:, n] = up.reshape(owners, places, channels).astype(out_ref.dtype)


def upstream_for_owners(x, c, owners):
    blocks, size, channels = x.shape
    row = pl.BlockSpec((MANY, size, channels), lambda b: (b, 0, 0))
    return pl.pallas_call(
        upstream_kernel,
        grid=(blocks // MANY,),
        in_specs=[row, row],
        out_specs=pl.BlockSpec((owners, MANY, size // owners, channels), lambda b: (0, b, 0, 0)),
        out_shape=jax.ShapeDtypeStruct((owners, blocks, size // owners, channels), x.dtype),
        cost_estimate=pl.CostEstimate(
            flops=8 * x.size, bytes_accessed=6 * x.size, transcendentals=x.size
        ),
        compiler_params=ROOM,
        name="upstream",
    )(x, c)


def final_kernel(y_ref, slope_ref, folded_ref, out_ref):
    many, size, channels = out_ref.shape
    for n in range(many):
        y = y_ref[:, n].reshape(size, channels)
        out_ref[n] = folded_ref[n] + y * slope_ref[n]


def final(y, slope, folded):
    blocks, size, channels = slope.shape
    owners = y.shape[0]
    row = pl.BlockSpec((MANY, size, channels), lambda b: (b, 0, 0))
    return pl.pallas_call(
        final_kernel,
        grid=(blocks // MANY,),
        in_specs=[
            pl.BlockSpec((owners, MANY, size // owners, channels), lambda b: (0, b, 0, 0)),
            row,
            row,
        ],
        out_specs=row,
        out_shape=jax.ShapeDtypeStruct(slope.shape, slope.dtype),
        cost_estimate=pl.CostEstimate(
            flops=100_000 * y.size, bytes_accessed=8 * y.size, transcendentals=0
        ),
        compiler_params=ROOM,
        name="final",
    )(y, slope, folded)


def tie_kernel(*refs):
    del refs


def tie(*values):
    anywhere = [pl.BlockSpec(memory_space=pl.ANY)] * len(values)
    return pl.pallas_call(
        tie_kernel,
        in_specs=anywhere,
        out_specs=anywhere,
        out_shape=[jax.ShapeDtypeStruct(v.shape, v.dtype) for v in values],
        input_output_aliases={n: n for n in range(len(values))},
        cost_estimate=pl.CostEstimate(flops=0, bytes_accessed=0, transcendentals=0),
        compiler_params=ROOM,
        name="tie",
    )(*values)


def body(inputs, cotangent, first_factor, second_factor):
    sequences, tokens, channels = inputs.shape
    assert sequences == 1
    owners = lax.axis_size("seq")
    row_block, blocks, size1 = first_factor.shape
    places = size1 // owners
    mean_weight = 1.0 / (sequences * lax.axis_size("dp"))
    bf16, wide = jnp.bfloat16, dict(preferred_element_type=jnp.float32)
    x = inputs.reshape(blocks, size1, channels)
    c = cotangent.reshape(blocks, size1, channels)

    def exchange(value):
        return lax.all_to_all(value, "seq", 0, 0, tiled=True)

    def to_columns(value):
        return exchange(value).reshape(owners * blocks, places, channels)

    def by_owner(value):
        return value.reshape(blocks, owners, places, channels).transpose(1, 0, 2, 3)

    first = lax.all_gather(first_factor, "dp", axis=0, tiled=True)
    second = lax.all_gather(second_factor, "dp", axis=0, tiled=True)
    up_columns = to_columns(upstream_for_owners(x, c, owners))
    mixed = by_owner(jnp.einsum("ibk,bkd->bid", first, x, **wide).astype(bf16))
    up_columns, mixed = tie(up_columns, mixed)
    columns = to_columns(mixed)
    back_columns = jnp.einsum("ijk,ijd->kjd", second, up_columns, **wide).astype(bf16)
    columns, back_columns = tie(columns, back_columns)
    mixed_grad = exchange(back_columns.reshape(owners, blocks, places, channels))
    product = jnp.einsum("ijk,kjd->ijd", second, columns, **wide).astype(bf16)
    mixed_grad, product = tie(mixed_grad, product)
    output = exchange(product.reshape(owners, blocks, places, channels))
    mixed_grad = mixed_grad.transpose(1, 0, 2, 3).reshape(blocks, size1, channels)
    second_grad = lax.psum_scatter(
        jnp.einsum("ijd,kjd->ijk", up_columns, columns, **wide) * mean_weight,
        "dp",
        scatter_dimension=0,
        tiled=True,
    )
    folded = jnp.einsum("ibk,bid->bkd", first, mixed_grad, **wide).astype(bf16)
    x_wide = x.astype(jnp.float32)
    logistic = jax.nn.sigmoid(x_wide)
    slope = (c.astype(jnp.float32) * logistic * (1.0 + x_wide * (1.0 - logistic))).astype(bf16)
    first_grad = lax.psum_scatter(
        jnp.einsum("bid,bkd->ibk", mixed_grad, x, **wide) * mean_weight,
        "dp",
        scatter_dimension=0,
        tiled=True,
    )
    grad_input = final(output, slope, folded).reshape(inputs.shape)
    return (grad_input, first_grad, second_grad)


def solution(mesh):
    placed = P("dp", "seq", None)
    return jax.shard_map(
        body,
        mesh=mesh,
        in_specs=(placed,) * 4,
        out_specs=(placed,) * 3,
        check_vma=False,
    )
```

```python
import functools

import jax
import jax.numpy as jnp
from jax import lax
from jax.experimental import pallas as pl
from jax.experimental.pallas import tpu as pltpu
from jax.sharding import PartitionSpec as P

ROOM = pltpu.CompilerParams(vmem_limit_bytes=56 * 1024 * 1024)
STEPS = 2
WINDOW = 5
ANYWHERE = pl.BlockSpec(memory_space=pl.ANY)


def cost(values, reads, flops=1):
    size = values.shape[0] * values.shape[1] * values.shape[2]
    return pl.CostEstimate(
        flops=flops * size, bytes_accessed=2 * reads * size, transcendentals=0
    )


def upstream_kernel(at_ref, x_ref, c_ref, *refs):
    del at_ref
    out_ref = refs[-1]
    for n in range(out_ref.shape[0]):
        x, c = x_ref[n, 0].astype(jnp.float32), c_ref[n, 0].astype(jnp.float32)
        half = 0.5 * x
        out_ref[n] = (c * (half + half * jnp.tanh(half))).astype(out_ref.dtype)


def pick_kernel(at_ref, value_ref, *refs):
    del at_ref
    refs[-1][...] = value_ref[...].reshape(refs[-1].shape)


def piece_call(kernel, values, axis, at, after, name):
    sizes = values[0].shape
    blocks, places, channels = sizes[1 - axis], sizes[2], sizes[3]
    many = blocks // STEPS
    if axis:
        rows = pl.BlockSpec((many, 1, places, channels), lambda b, at: (b, at[0], 0, 0))
    else:
        rows = pl.BlockSpec((1, many, places, channels), lambda b, at: (at[0], b, 0, 0))
    out = jax.ShapeDtypeStruct((blocks, places, channels), values[0].dtype)
    return pl.pallas_call(
        kernel,
        grid_spec=pltpu.PrefetchScalarGridSpec(
            num_scalar_prefetch=1,
            grid=(STEPS,),
            in_specs=[rows] * len(values) + [ANYWHERE] * len(after),
            out_specs=pl.BlockSpec((many, places, channels), lambda b, at: (b, 0, 0)),
        ),
        out_shape=out,
        cost_estimate=cost(out, 1 + len(values)),
        compiler_params=ROOM,
        name=name,
    )(at, *values, *after)


def final_kernel(at_ref, y_ref, slope_ref, folded_ref, *refs):
    del at_ref
    out_ref = refs[-1]
    for n in range(out_ref.shape[0]):
        out_ref[n, 0] = folded_ref[n, 0] + y_ref[n] * slope_ref[n, 0]


def final_piece(y, slope, folded, so_far, at, after):
    blocks, _, places, channels = slope.shape
    many = blocks // STEPS
    rows = pl.BlockSpec((many, 1, places, channels), lambda b, at: (b, at[0], 0, 0))
    piece = pl.BlockSpec((many, places, channels), lambda b, at: (b, 0, 0))
    before = ([] if so_far is None else [so_far]) + after
    return pl.pallas_call(
        final_kernel,
        grid_spec=pltpu.PrefetchScalarGridSpec(
            num_scalar_prefetch=1,
            grid=(STEPS,),
            in_specs=[piece, rows, rows] + [ANYWHERE] * len(before),
            out_specs=rows,
        ),
        out_shape=jax.ShapeDtypeStruct(slope.shape, slope.dtype),
        input_output_aliases={} if so_far is None else {4: 0},
        cost_estimate=cost(y, 4, 100_000),
        compiler_params=ROOM,
        name="final",
    )(at, y, slope, folded, *before)


def place_kernel(owners, where_ref, *refs):
    del where_ref
    out_ref = refs[-1]
    for d in range(owners):

        @pl.when(pl.program_id(0) == d)
        def _():
            out_ref[...] = refs[d][...].reshape(out_ref.shape)


def place(pieces, where, axis, after):
    blocks, places, channels = pieces[0].shape
    owners = len(pieces)
    if axis:
        shape, block = (blocks, owners, places, channels), (blocks, 1, places, channels)
        spec = pl.BlockSpec(block, lambda d, where: (0, where[0] ^ d, 0, 0))
    else:
        shape, block = (owners, blocks, places, channels), (1, blocks, places, channels)
        spec = pl.BlockSpec(block, lambda d, where: (where[0] ^ d, 0, 0, 0))
    whole = pl.BlockSpec((blocks, places, channels), lambda d, where: (0, 0, 0))
    return pl.pallas_call(
        functools.partial(place_kernel, owners),
        grid_spec=pltpu.PrefetchScalarGridSpec(
            num_scalar_prefetch=1,
            grid=(owners,),
            in_specs=[whole] * owners + [ANYWHERE] * len(after),
            out_specs=spec,
        ),
        out_shape=jax.ShapeDtypeStruct(shape, pieces[0].dtype),
        cost_estimate=cost(pieces[0], 2 * owners),
        compiler_params=ROOM,
        name="place",
    )(where, *pieces, *after)


def tie_kernel(*refs):
    del refs


def tie(value, after):
    return pl.pallas_call(
        tie_kernel,
        in_specs=[ANYWHERE] * (1 + len(after)),
        out_specs=ANYWHERE,
        out_shape=jax.ShapeDtypeStruct(value.shape, value.dtype),
        input_output_aliases={0: 0},
        cost_estimate=pl.CostEstimate(flops=0, bytes_accessed=0, transcendentals=0),
        compiler_params=ROOM,
        name="tie",
    )(value, *after)


def body(inputs, cotangent, first_factor, second_factor):
    sequences, tokens, channels = inputs.shape
    assert sequences == 1
    owners = lax.axis_size("seq")
    row_block, blocks, size1 = first_factor.shape
    places = size1 // owners
    mean_weight = 1.0 / (sequences * lax.axis_size("dp"))
    bf16, wide = jnp.bfloat16, dict(preferred_element_type=jnp.float32)
    me = lax.axis_index("seq").astype(jnp.int32)
    where = [(me ^ d).reshape(1) for d in range(owners)]
    rows = (blocks, owners, places, channels)
    columns_first = (owners, blocks, places, channels)
    column_shape = (owners * blocks, places, channels)
    x_rows, c_rows = inputs.reshape(rows), cotangent.reshape(rows)
    x = inputs.reshape(blocks, size1, channels)
    distances = [owners // 2]
    for d in range(1, owners // 2):
        distances += [d, owners // 2 + d]
    line, cuts = [], []

    def exchange(kernel, values, axis, name, order, between=None):
        got = {}
        for k, d in enumerate(order):
            after = cuts[-1:] + (line[-WINDOW:][:1] if len(line) >= WINDOW else [])
            if k == WINDOW and between is not None:
                after += between(cuts[-1])
            cuts.append(piece_call(kernel, values, axis, where[d], after, name))
            got[d] = lax.ppermute(cuts[-1], "seq", [(n, n ^ d) for n in range(owners)])
            line.append(got[d])
        got[0] = piece_call(kernel, values, axis, where[0], [], name)
        return [got[d] for d in range(owners)]

    first = lax.all_gather(first_factor, "dp", axis=0, tiled=True)
    second = lax.all_gather(second_factor, "dp", axis=0, tiled=True)
    made = {}

    def to_back(cut):
        made["up"] = place(up_pieces, where[0], 0, []).reshape(column_shape)
        back = jnp.einsum("ijk,ijd->kjd", second, made["up"], **wide).astype(bf16)
        made["back"] = back.reshape(columns_first)
        return [made["back"]]

    def to_product(cut):
        made["columns"] = place(mixed_pieces, where[0], 0, []).reshape(column_shape)
        product = jnp.einsum("ijk,kjd->ijd", second, made["columns"], **wide).astype(bf16)
        made["product"] = product.reshape(columns_first)
        return [made["product"]]

    def to_folded(cut):
        mixed_grad = place(grad_pieces, where[0], 1, []).reshape(blocks, size1, channels)
        made["first"] = jnp.einsum("bid,bkd->ibk", mixed_grad, x, **wide) * mean_weight
        folded = jnp.einsum("ibk,bid->bkd", first, mixed_grad, **wide).astype(bf16)
        made["folded"] = folded.reshape(rows)
        return [made["folded"], made["first"]]

    up_pieces = exchange(upstream_kernel, [x_rows, c_rows], 1, "upstream", distances)
    mixed = jnp.einsum("ibk,bkd->bid", first, x, **wide).astype(bf16).reshape(rows)
    mixed_pieces = exchange(pick_kernel, [mixed], 1, "pick", distances, to_back)
    grad_pieces = exchange(pick_kernel, [made["back"]], 0, "pick", distances, to_product)
    columns = made["columns"]
    second_grad = lax.psum_scatter(
        jnp.einsum("ijd,kjd->ijk", made["up"], columns, **wide) * mean_weight,
        "dp",
        scatter_dimension=0,
        tiled=True,
    )
    output = exchange(pick_kernel, [made["product"]], 0, "pick", distances, to_folded)
    first_grad = lax.psum_scatter(made["first"], "dp", scatter_dimension=0, tiled=True)
    x_wide = x.astype(jnp.float32)
    c_wide = cotangent.reshape(x.shape).astype(jnp.float32)
    logistic = jax.nn.sigmoid(x_wide)
    slope = (c_wide * logistic * (1.0 + x_wide * (1.0 - logistic))).astype(bf16)
    slope, grad_input = slope.reshape(rows), None
    for d in [0] + distances:
        after = [first_grad, second_grad] if d == distances[-2] else []
        grad_input = final_piece(output[d], slope, made["folded"], grad_input, where[d], after)
    grad_input = grad_input.reshape(inputs.shape)
    return (grad_input, first_grad, second_grad)


def solution(mesh):
    placed = P("dp", "seq", None)
    return jax.shard_map(
        body,
        mesh=mesh,
        in_specs=(placed,) * 4,
        out_specs=(placed,) * 3,
        check_vma=False,
    )
```

```python
import functools

import jax
import jax.numpy as jnp
from jax import lax
from jax.experimental import pallas as pl
from jax.experimental.pallas import tpu as pltpu
from jax.sharding import PartitionSpec as P

ROOM = pltpu.CompilerParams(vmem_limit_bytes=56 * 1024 * 1024)
STEPS = 2
WINDOW = 6
ANYWHERE = pl.BlockSpec(memory_space=pl.ANY)


def cost(values, reads, flops=1):
    size = values.shape[0] * values.shape[1] * values.shape[2]
    return pl.CostEstimate(
        flops=flops * size, bytes_accessed=2 * reads * size, transcendentals=0
    )


def upstream_kernel(at_ref, x_ref, c_ref, *refs):
    del at_ref
    out_ref = refs[-1]
    for n in range(out_ref.shape[0]):
        x, c = x_ref[n, 0].astype(jnp.float32), c_ref[n, 0].astype(jnp.float32)
        half = 0.5 * x
        out_ref[n] = (c * (half + half * jnp.tanh(half))).astype(out_ref.dtype)


def pick_kernel(at_ref, value_ref, *refs):
    del at_ref
    refs[-1][...] = value_ref[...].reshape(refs[-1].shape)


def piece_call(kernel, values, axis, at, after, name):
    sizes = values[0].shape
    blocks, places, channels = sizes[1 - axis], sizes[2], sizes[3]
    many = blocks // STEPS
    if axis:
        rows = pl.BlockSpec((many, 1, places, channels), lambda b, at: (b, at[0], 0, 0))
    else:
        rows = pl.BlockSpec((1, many, places, channels), lambda b, at: (at[0], b, 0, 0))
    out = jax.ShapeDtypeStruct((blocks, places, channels), values[0].dtype)
    return pl.pallas_call(
        kernel,
        grid_spec=pltpu.PrefetchScalarGridSpec(
            num_scalar_prefetch=1,
            grid=(STEPS,),
            in_specs=[rows] * len(values) + [ANYWHERE] * len(after),
            out_specs=pl.BlockSpec((many, places, channels), lambda b, at: (b, 0, 0)),
        ),
        out_shape=out,
        cost_estimate=cost(out, 1 + len(values)),
        compiler_params=ROOM,
        name=name,
    )(at, *values, *after)


def final_kernel(at_ref, y_ref, slope_ref, folded_ref, *refs):
    del at_ref
    out_ref = refs[-1]
    for n in range(out_ref.shape[0]):
        out_ref[n, 0] = folded_ref[n, 0] + y_ref[n] * slope_ref[n, 0]


def final_piece(y, slope, folded, so_far, at, after):
    blocks, _, places, channels = slope.shape
    many = blocks // STEPS
    rows = pl.BlockSpec((many, 1, places, channels), lambda b, at: (b, at[0], 0, 0))
    piece = pl.BlockSpec((many, places, channels), lambda b, at: (b, 0, 0))
    before = ([] if so_far is None else [so_far]) + after
    return pl.pallas_call(
        final_kernel,
        grid_spec=pltpu.PrefetchScalarGridSpec(
            num_scalar_prefetch=1,
            grid=(STEPS,),
            in_specs=[piece, rows, rows] + [ANYWHERE] * len(before),
            out_specs=rows,
        ),
        out_shape=jax.ShapeDtypeStruct(slope.shape, slope.dtype),
        input_output_aliases={} if so_far is None else {4: 0},
        cost_estimate=cost(y, 4, 100_000),
        compiler_params=ROOM,
        name="final",
    )(at, y, slope, folded, *before)


def place_kernel(owners, where_ref, *refs):
    del where_ref
    out_ref = refs[-1]
    for d in range(owners):

        @pl.when(pl.program_id(0) == d)
        def _():
            out_ref[...] = refs[d][...].reshape(out_ref.shape)


def place(pieces, where, axis, after):
    blocks, places, channels = pieces[0].shape
    owners = len(pieces)
    if axis:
        shape, block = (blocks, owners, places, channels), (blocks, 1, places, channels)
        spec = pl.BlockSpec(block, lambda d, where: (0, where[0] ^ d, 0, 0))
    else:
        shape, block = (owners, blocks, places, channels), (1, blocks, places, channels)
        spec = pl.BlockSpec(block, lambda d, where: (where[0] ^ d, 0, 0, 0))
    whole = pl.BlockSpec((blocks, places, channels), lambda d, where: (0, 0, 0))
    return pl.pallas_call(
        functools.partial(place_kernel, owners),
        grid_spec=pltpu.PrefetchScalarGridSpec(
            num_scalar_prefetch=1,
            grid=(owners,),
            in_specs=[whole] * owners + [ANYWHERE] * len(after),
            out_specs=spec,
        ),
        out_shape=jax.ShapeDtypeStruct(shape, pieces[0].dtype),
        cost_estimate=cost(pieces[0], 2 * owners),
        compiler_params=ROOM,
        name="place",
    )(where, *pieces, *after)


def tie_kernel(*refs):
    del refs


def tie(value, after):
    return pl.pallas_call(
        tie_kernel,
        in_specs=[ANYWHERE] * (1 + len(after)),
        out_specs=ANYWHERE,
        out_shape=jax.ShapeDtypeStruct(value.shape, value.dtype),
        input_output_aliases={0: 0},
        cost_estimate=pl.CostEstimate(flops=0, bytes_accessed=0, transcendentals=0),
        compiler_params=ROOM,
        name="tie",
    )(value, *after)


def body(inputs, cotangent, first_factor, second_factor):
    sequences, tokens, channels = inputs.shape
    assert sequences == 1
    owners = lax.axis_size("seq")
    row_block, blocks, size1 = first_factor.shape
    places = size1 // owners
    mean_weight = 1.0 / (sequences * lax.axis_size("dp"))
    bf16, wide = jnp.bfloat16, dict(preferred_element_type=jnp.float32)
    me = lax.axis_index("seq").astype(jnp.int32)
    where = [(me ^ d).reshape(1) for d in range(owners)]
    rows = (blocks, owners, places, channels)
    columns_first = (owners, blocks, places, channels)
    column_shape = (owners * blocks, places, channels)
    x_rows, c_rows = inputs.reshape(rows), cotangent.reshape(rows)
    x = inputs.reshape(blocks, size1, channels)
    distances = [owners // 2]
    for d in range(1, owners // 2):
        distances += [d, owners // 2 + d]
    line, cuts = [], []

    def exchange(kernel, values, axis, name, order, between=None):
        got = {}
        for k, d in enumerate(order):
            after = cuts[-1:] + (line[-WINDOW:][:1] if len(line) >= WINDOW else [])
            if k == WINDOW and between is not None:
                after += between(cuts[-1])
            cuts.append(piece_call(kernel, values, axis, where[d], after, name))
            got[d] = lax.ppermute(cuts[-1], "seq", [(n, n ^ d) for n in range(owners)])
            line.append(got[d])
        got[0] = piece_call(kernel, values, axis, where[0], [], name)
        return [got[d] for d in range(owners)]

    first = lax.all_gather(first_factor, "dp", axis=0, tiled=True)
    second = lax.all_gather(second_factor, "dp", axis=0, tiled=True)
    made = {}

    def to_slope(cut):
        x_wide = x.astype(jnp.float32)
        c_wide = cotangent.reshape(x.shape).astype(jnp.float32)
        logistic = jax.nn.sigmoid(x_wide)
        slope = (c_wide * logistic * (1.0 + x_wide * (1.0 - logistic))).astype(bf16)
        made["slope"] = slope
        return [slope]

    def to_back(cut):
        made["up"] = place(up_pieces, where[0], 0, []).reshape(column_shape)
        back = jnp.einsum("ijk,ijd->kjd", second, made["up"], **wide).astype(bf16)
        made["back"] = back.reshape(columns_first)
        return [made["back"]]

    def to_product(cut):
        made["columns"] = place(mixed_pieces, where[0], 0, []).reshape(column_shape)
        product = jnp.einsum("ijk,kjd->ijd", second, made["columns"], **wide).astype(bf16)
        made["product"] = product.reshape(columns_first)
        return [made["product"]]

    def to_folded(cut):
        mixed_grad = place(grad_pieces, where[0], 1, []).reshape(blocks, size1, channels)
        made["first"] = jnp.einsum("bid,bkd->ibk", mixed_grad, x, **wide) * mean_weight
        folded = jnp.einsum("ibk,bid->bkd", first, mixed_grad, **wide).astype(bf16)
        made["folded"] = folded.reshape(rows)
        return [made["folded"], made["first"]]

    up_pieces = exchange(upstream_kernel, [x_rows, c_rows], 1, "upstream", distances, to_slope)
    mixed = jnp.einsum("ibk,bkd->bid", first, x, **wide).astype(bf16).reshape(rows)
    mixed_pieces = exchange(pick_kernel, [mixed], 1, "pick", distances, to_back)
    grad_pieces = exchange(pick_kernel, [made["back"]], 0, "pick", distances, to_product)
    columns = made["columns"]
    second_grad = lax.psum_scatter(
        jnp.einsum("ijd,kjd->ijk", made["up"], columns, **wide) * mean_weight,
        "dp",
        scatter_dimension=0,
        tiled=True,
    )
    output = exchange(pick_kernel, [made["product"]], 0, "pick", distances, to_folded)
    first_grad = lax.psum_scatter(made["first"], "dp", scatter_dimension=0, tiled=True)
    slope, grad_input = made["slope"].reshape(rows), None
    for d in [0] + distances:
        after = [first_grad, second_grad] if d == distances[-2] else []
        grad_input = final_piece(output[d], slope, made["folded"], grad_input, where[d], after)
    grad_input = grad_input.reshape(inputs.shape)
    return (grad_input, first_grad, second_grad)


def solution(mesh):
    placed = P("dp", "seq", None)
    return jax.shard_map(
        body,
        mesh=mesh,
        in_specs=(placed,) * 4,
        out_specs=(placed,) * 3,
        check_vma=False,
    )
```
